32 devices in a mesh: fsdp: 32 (over z, y, x, core).
Axes of the slice: x: 2, y: 2, z: 4, core: 2. Of those that a mesh axis runs over, the one named last changes fastest.
Arguments:
- hidden_in: bfloat16 [32768, 768], P('fsdp'), may hold values from -6 to 6
- segment_ids: int32 [32768], P('fsdp'), may hold values from -1 to 543, as said below
- project_in: bfloat16 [2304, 768], P('fsdp'), may hold values from -0.21875 to 0.21875
- project_out: bfloat16 [768, 768], P('fsdp'), may hold values from -0.625 to 0.625
- expand_weight: bfloat16 [2304, 768], P('fsdp'), may hold values from -0.21875 to 0.21875
- shrink_weight: bfloat16 [768, 1152], P('fsdp'), may hold values from -0.1875 to 0.1875
- first_gain: bfloat16 [768], P('fsdp'), may hold values from 0.5 to 1.5
- second_gain: bfloat16 [768], P('fsdp'), may hold values from 0.5 to 1.5
- cotangent: bfloat16 [32768, 768], P('fsdp'), may hold values from -6 to 6
Outputs:
- hidden_out: bfloat16 [32768, 768], P('fsdp')
- grad_input: bfloat16 [32768, 768], P('fsdp')
- grad_project_in: float32 [2304, 768], P('fsdp')
- grad_project_out: float32 [768, 768], P('fsdp')
- grad_expand: float32 [2304, 768], P('fsdp')
- grad_shrink: float32 [768, 1152], P('fsdp')
- grad_first_gain: float32 [768], P('fsdp')
- grad_second_gain: float32 [768], P('fsdp')
The draws below stay inside these ranges and needn't reach their ends.
Inputs may be any that keep to these rules, and one draw needn't show every extreme that they name: `segment_ids`: within each aligned block of 1024 slots, equal numbers form one run (one sequence of at most 512 tokens); -1 marks padding, which stands only at the end of a block; runs of different blocks carry different numbers. Some sequence has exactly 512 tokens, and some block has no padding.
All inputs are finite; a program needn't handle non-finite values.
Results may differ from the reference program's by a relative error of at most 0.01.
Values may be sent and summed in bfloat16 or wider, within the bound.
A program may use at most 320 MiB of HBM per device.

```python
import jax
import jax.numpy as jnp
from jax import lax

D = 768
HEADS = 12
HEAD_DIM = 64
FF = 1152
TOK_DEV = 1024
SEQ_MAX = 512
TOKENS = 32768


def draw_segment_ids(key, part):
    key = jax.random.fold_in(key, 7)
    block_count = TOKENS // TOK_DEV
    shortest = SEQ_MAX // 8
    per_block = TOK_DEV // shortest + 1
    key_len, key_fill, key_pick = jax.random.split(key, 3)
    lengths = jax.random.randint(key_len, (block_count, per_block), shortest, SEQ_MAX + 1)
    chosen = jax.random.randint(key_pick, (), 0, block_count)
    is_chosen = jnp.arange(block_count) == chosen
    lengths = lengths.at[:, 0].set(jnp.where(is_chosen, SEQ_MAX, lengths[:, 0]))
    filled = jax.random.randint(key_fill, (block_count,), TOK_DEV // 2, TOK_DEV + 1)
    filled = jnp.where(is_chosen, TOK_DEV, filled)
    ends = jnp.cumsum(lengths, axis=1)
    position = jnp.arange(TOK_DEV)
    local = jnp.sum((ends[:, None, :] <= position[None, :, None]).astype(jnp.int32), axis=-1)
    numbers = jnp.arange(block_count)[:, None] * per_block + local
    numbers = jnp.where(position[None, :] < filled[:, None], numbers, -1)
    return numbers.reshape(TOKENS).astype(jnp.int32)


def spiked(result, key, source, target, parts, factor):
    owner, partner = [(jnp.arange(result.shape[axis_at]) // (result.shape[axis_at] // parts)).reshape([-1 if axis == axis_at else 1 for axis in range(result.ndim)]) for axis_at in (source, target)]
    chosen = jax.random.permutation(key, parts)[partner]
    strong = (owner == chosen) | (owner == (partner + parts // 2) % parts)
    return jnp.where(strong, factor * result, result)


def shard_levels(rng, extent, shards, least, high):
    loudness, own = 1.0, jax.random.fold_in(rng, 6)
    for axis_at, parts in shards:
        steps = jnp.exp(jax.random.uniform(jax.random.fold_in(own, axis_at), (parts,), jnp.float32, least / len(shards), high / len(shards)))
        loudness = loudness * jnp.repeat(steps, extent[axis_at] // parts).reshape([-1 if axis == axis_at else 1 for axis in range(len(extent))])
    return loudness


def normal_values(rng, extent, width, bound, cuts=(), held_as=jnp.bfloat16):
    loudness = shard_levels(rng, extent, cuts, -0.22, 0.18) if cuts else 1.0
    entries = jax.random.normal(rng, extent, jnp.float32) * width * loudness
    return jnp.minimum(jnp.maximum(entries, -bound), bound).astype(held_as)


def gaussian_with(key, shape, scale, bound, shards, heavy, kind=jnp.bfloat16):
    values = scale * jax.random.normal(key, shape, jnp.float32)
    if shards:
        values = values * shard_levels(key, shape, shards, -0.22, 0.18)
    return jnp.clip(spiked(values, jax.random.fold_in(key, 3), *heavy), -bound, bound).astype(kind)


def setup_inputs(seed: int = 0) -> dict:
    keys = jax.random.split(jax.random.key(seed), 10)
    return {
        "hidden_in": normal_values(keys[0], (TOKENS, D), 1.0, 6.0, ((0, 32),)),
        "segment_ids": draw_segment_ids(jax.random.fold_in(keys[9], 71), 0),
        "project_in": normal_values(keys[2], (3 * D, D), D ** -0.5, 0.21875, ((0, 32),)),
        "project_out": normal_values(keys[3], (D, D), (D // 8) ** -0.5, 0.625, ((0, 32),)),
        "expand_weight": normal_values(keys[4], (2 * FF, D), D ** -0.5, 0.21875, ((0, 32),)),
        "shrink_weight": normal_values(keys[5], (D, FF), FF ** -0.5, 0.1875, ((0, 32),)),
        "first_gain": jnp.clip(1.0 + 0.1 * jax.random.normal(keys[6], (D,), jnp.float32), 0.5, 1.5).astype(jnp.bfloat16),
        "second_gain": jnp.clip(1.0 + 0.1 * jax.random.normal(keys[7], (D,), jnp.float32), 0.5, 1.5).astype(jnp.bfloat16),
        "cotangent": gaussian_with(keys[8], (TOKENS, D), 1.0, 6.0, ((0, 32),), (0, 1, 32, 2.75)),
    }


eps_norm = 1e-05
rope_base = 160000.0
masked_score = -1e+30

@jax.custom_vjp
def low(v):
    return lax.optimization_barrier(v.astype(jnp.bfloat16)).astype(jnp.float32)

@jax.custom_vjp
def low_back(v):
    return v

def low_keep(v):
    return (low(v), None)

def low_pass(kept, grad):
    return (grad,)

def back_keep(v):
    return (v, None)

def back_low(kept, grad):
    return (low(grad),)
low.defvjp(low_keep, low_pass)
low_back.defvjp(back_keep, back_low)

def layer_norm(values, gain):
    center = lax.optimization_barrier(jnp.mean(values, axis=-1, keepdims=True))
    centred = values - center
    spread = lax.optimization_barrier(jnp.mean(centred * centred, axis=-1, keepdims=True))
    return centred * lax.rsqrt(spread + eps_norm) * gain

def rotate_half(values):
    middle_index = values.shape[-1] // 2
    return jnp.concatenate([-values[..., middle_index:], values[..., :middle_index]], axis=-1)

def rope_tables(segment_ids, head_size):
    slot_count = segment_ids.shape[0]
    slots = jnp.arange(slot_count, dtype=jnp.int32)
    changed = jnp.concatenate([jnp.ones((1,), dtype=bool), segment_ids[1:] != segment_ids[:-1]])
    starts = lax.cummax(jnp.where(changed, slots, jnp.zeros_like(slots)), axis=0)
    position = (slots - starts).astype(jnp.float32)
    freq = rope_base ** (-jnp.arange(head_size // 2, dtype=jnp.float32) * 2.0 / head_size)
    angle = position[:, None] * freq[None, :]
    angle = jnp.concatenate([angle, angle], axis=-1)
    return (jnp.cos(angle), jnp.sin(angle))

def apply_rope(values, cosine, sine):
    return values * cosine[:, None, :] + rotate_half(values) * sine[:, None, :]

def block_forward(hidden, segment_ids, project_in, project_out, expand_weight, shrink_weight, first_gain, second_gain):
    highest = lax.Precision.HIGHEST
    slot_count = hidden.shape[0]
    normed = low(layer_norm(hidden, first_gain))
    joined = low_back(jnp.dot(normed, project_in.T, precision=highest))
    cosine, sine = rope_tables(segment_ids, HEAD_DIM)
    queries = low(apply_rope(joined[:, :D].reshape(slot_count, HEADS, HEAD_DIM), cosine, sine))
    keys_rot = low(apply_rope(joined[:, D:2 * D].reshape(slot_count, HEADS, HEAD_DIM), cosine, sine))
    values_low = low(joined[:, 2 * D:].reshape(slot_count, HEADS, HEAD_DIM))
    slots = jnp.arange(slot_count, dtype=jnp.int32)
    same_seq = (segment_ids[:, None] == segment_ids[None, :]) & (segment_ids[:, None] >= 0)
    allowed = same_seq | (slots[:, None] == slots[None, :])
    scores = low_back(jnp.einsum('qhd,khd->hqk', queries, keys_rot, precision=highest) * HEAD_DIM ** (-0.5))
    scores = jnp.where(allowed[None], scores, masked_score)
    row_peak = lax.optimization_barrier(jnp.max(scores, axis=-1, keepdims=True))
    shifted = jnp.exp(scores - row_peak)
    probs = low(shifted / lax.optimization_barrier(jnp.sum(shifted, axis=-1, keepdims=True)))
    mixed = jnp.einsum('hqk,khd->qhd', probs, values_low, precision=highest).reshape(slot_count, D)
    mixed = low(low_back(mixed))
    attended = low_back(jnp.dot(mixed, project_out.T, precision=highest))
    middle = hidden + attended
    normed_two = low(layer_norm(middle, second_gain))
    widened = low_back(jnp.dot(normed_two, expand_weight.T, precision=highest))
    product = low(jax.nn.gelu(widened[:, :FF], approximate=False) * widened[:, FF:])
    return middle + jnp.dot(product, shrink_weight.T, precision=highest)

def reference(hidden_in, segment_ids, project_in, project_out, expand_weight, shrink_weight, first_gain, second_gain, cotangent):
    floats = tuple((array.astype(jnp.float32) for array in (hidden_in, project_in, project_out, expand_weight, shrink_weight, first_gain, second_gain)))
    segments = segment_ids.reshape(-1, TOK_DEV)

    def whole(hidden, weight_in, weight_out, weight_expand, weight_shrink, gain_one, gain_two):

        def one_block(packed):
            return block_forward(packed[0], packed[1], weight_in, weight_out, weight_expand, weight_shrink, gain_one, gain_two)
        return lax.map(jax.checkpoint(one_block), (hidden.reshape(-1, TOK_DEV, D), segments))
    output, backward = jax.vjp(whole, *floats)
    grads = backward(cotangent.astype(jnp.float32).reshape(-1, TOK_DEV, D))
    return (output.reshape(TOKENS, D).astype(jnp.bfloat16), grads[0].reshape(TOKENS, D).astype(jnp.bfloat16), grads[1], grads[2], grads[3], grads[4], grads[5], grads[6])
```

```python
import functools

import jax
import jax.numpy as jnp
from jax import lax
from jax.experimental import pallas as pl
from jax.experimental.pallas import tpu as pltpu
from jax.sharding import PartitionSpec as P

D = 768
HEADS = 12
HEAD_DIM = 64
FF = 1152


eps_norm = 1e-05
rope_base = 160000.0
masked_score = -1e30


def layer_norm(values, gain):
    center = jnp.mean(values, axis=-1, keepdims=True)
    centred = values - center
    spread = jnp.mean(centred * centred, axis=-1, keepdims=True)
    return centred * lax.rsqrt(spread + eps_norm) * gain


def gated_gelu(gate, upward):
    return jax.nn.gelu(gate, approximate=False) * upward


BQ = 256
PAIR = 2 * HEAD_DIM
STEP = 128


def swap_halves(values):
    lane = lax.broadcasted_iota(jnp.int32, values.shape, 1)
    low_half = lane % HEAD_DIM < HEAD_DIM // 2
    up = pltpu.roll(values, PAIR - HEAD_DIM // 2, 1)
    down = pltpu.roll(values, HEAD_DIM // 2, 1)
    return jnp.where(low_half, up, down)


def dot_nt(left, right):
    return lax.dot_general(
        left, right, (((1,), (1,)), ((), ())), preferred_element_type=jnp.float32
    )


def dot_nn(left, right):
    return jnp.dot(left, right, preferred_element_type=jnp.float32)


def attend_kernel(
    lo_ref, width_ref, q_ref, k_ref, v_ref, cos_ref, sin_ref, code_row_ref, code_col_ref,
    qr_ref, kr_ref, vr_ref, mixed_ref, lse_ref, vt_ref,
):
    number = pl.program_id(1)
    total = k_ref.shape[0]

    @pl.when(number == 0)
    def _():
        keys = k_ref[...]
        kr_ref[...] = (keys * cos_ref[...] + swap_halves(keys) * sin_ref[...]).astype(jnp.bfloat16)
        vr_ref[...] = v_ref[...].astype(jnp.bfloat16)
        vt_ref[...] = v_ref[...].T.astype(jnp.bfloat16)

    rows = pl.ds(pl.multiple_of(number * BQ, BQ), BQ)
    queries = q_ref[...]
    queries = queries * cos_ref[rows, :] + swap_halves(queries) * sin_ref[rows, :]
    queries = queries.astype(jnp.bfloat16) * jnp.bfloat16(HEAD_DIM**-0.5)
    qr_ref[...] = queries
    start = pl.multiple_of(lo_ref[number] * STEP, STEP)

    for quarter in range(1, total // BQ + 1):
        width = quarter * BQ

        @pl.when(width_ref[number] == quarter)
        def _():
            window = pl.ds(start, width)
            allowed = code_col_ref[window, :1] == code_row_ref[:1, :]
            outs = []
            for side in range(2):
                part = slice(side * HEAD_DIM, (side + 1) * HEAD_DIM)
                scores = dot_nt(kr_ref[window, part], queries[:, part])
                scores = jnp.where(allowed, scores, masked_score)
                peak = jnp.max(scores, axis=0, keepdims=True)
                shifted = jnp.exp(scores - peak)
                amount = jnp.sum(shifted, axis=0, keepdims=True)
                lse_ref[0, side : side + 1, :] = peak + jnp.log(amount)
                out = dot_nn(vt_ref[part, window], shifted.astype(jnp.bfloat16))
                outs.append(out * (1.0 / amount))
            mixed_ref[...] = jnp.concatenate(outs, axis=0).T.astype(jnp.bfloat16)


def attend_back_kernel(
    lo_ref, width_ref, qr_ref, kr_ref, vr_ref, gm_ref, lse_ref, cos_ref, sin_ref,
    code_row_ref, code_col_ref, gq_ref, gk_ref, gv_ref, kt_ref, gk_sum, gv_sum,
):
    number = pl.program_id(1)
    total = kr_ref.shape[0]

    @pl.when(number == 0)
    def _():
        kt_ref[...] = kr_ref[...].astype(jnp.float32).T.astype(jnp.bfloat16)
        gk_sum[...] = jnp.zeros_like(gk_sum)
        gv_sum[...] = jnp.zeros_like(gv_sum)

    rows = pl.ds(pl.multiple_of(number * BQ, BQ), BQ)
    queries = qr_ref[...]
    grads = gm_ref[...]
    start = pl.multiple_of(lo_ref[number] * STEP, STEP)

    for quarter in range(1, total // BQ + 1):
        width = quarter * BQ

        @pl.when(width_ref[number] == quarter)
        def _():
            window = pl.ds(start, width)
            allowed = code_col_ref[window, :1] == code_row_ref[:1, :]
            outs, key_parts, value_parts = [], [], []
            for side in range(2):
                part = slice(side * HEAD_DIM, (side + 1) * HEAD_DIM)
                scores = dot_nt(kr_ref[window, part], queries[:, part])
                scores = jnp.where(allowed, scores, masked_score)
                probs = jnp.exp(scores - lse_ref[0, side : side + 1, :])
                value_parts.append(dot_nn(probs.astype(jnp.bfloat16), grads[:, part]))
                weighted = probs * dot_nt(vr_ref[window, part], grads[:, part])
                row_dot = jnp.sum(weighted, axis=0, keepdims=True)
                grad_scores = (weighted - probs * row_dot).astype(jnp.bfloat16)
                key_parts.append(dot_nn(grad_scores, queries[:, part]))
                outs.append(dot_nn(kt_ref[part, window], grad_scores))
            gv_sum[window, :] += jnp.concatenate(value_parts, axis=1)
            gk_sum[window, :] += jnp.concatenate(key_parts, axis=1)
            out = jnp.concatenate(outs, axis=0).T * HEAD_DIM**-0.5
            gq_ref[...] = (
                out * cos_ref[rows, :] - swap_halves(out) * sin_ref[rows, :]
            ).astype(jnp.bfloat16)

    @pl.when(number == pl.num_programs(1) - 1)
    def _():
        keys = gk_sum[...]
        gk_ref[...] = (keys * cos_ref[...] - swap_halves(keys) * sin_ref[...]).astype(jnp.bfloat16)
        gv_ref[...] = gv_sum[...].astype(jnp.bfloat16)


def attention_tables(segment_ids):
    slot_count = segment_ids.shape[0]
    slots = jnp.arange(slot_count, dtype=jnp.int32)
    same = segment_ids[:, None] == segment_ids[None, :]
    starts = jnp.min(jnp.where(same, slots[None, :], slot_count), axis=1)
    ends = jnp.max(jnp.where(same, slots[None, :], -1), axis=1) + 1
    padding = segment_ids < 0
    code = jnp.where(padding, -1 - slots, segment_ids)
    first = jnp.where(padding, slots, starts)[::BQ] // STEP
    last = (jnp.where(padding, slots + 1, ends)[BQ - 1 :: BQ] + STEP - 1) // STEP
    ratio = BQ // STEP
    width = (last - first + ratio - 1) // ratio
    lo = jnp.minimum(first, slot_count // STEP - ratio * width)
    position = (slots - starts).astype(jnp.float32)
    lane = jnp.arange(PAIR, dtype=jnp.int32)
    half = HEAD_DIM // 2
    freq = rope_base ** (-(lane % half).astype(jnp.float32) * 2.0 / HEAD_DIM)
    angle = position[:, None] * freq[None, :]
    sign = jnp.where(lane % HEAD_DIM < half, -1.0, 1.0)
    code_row = jnp.broadcast_to(code[None, :], (8, slot_count))
    code_col = jnp.broadcast_to(code[:, None], (slot_count, STEP))
    return lo, width, jnp.cos(angle), jnp.sin(angle) * sign[None, :], code_row, code_col


def table_specs(slot_count):
    return (
        [pl.BlockSpec((slot_count, PAIR), lambda h, i, *_: (0, 0))] * 2,
        [
            pl.BlockSpec((8, BQ), lambda h, i, *_: (0, i)),
            pl.BlockSpec((slot_count, STEP), lambda h, i, *_: (0, 0)),
        ],
    )


def attend(joined, tables):
    lo, width, cosine, sine, code_row, code_col = tables
    slot_count = joined.shape[0]
    pairs = D // PAIR
    rope_specs, code_specs = table_specs(slot_count)
    block = pl.BlockSpec((BQ, PAIR), lambda h, i, *_: (i, h))
    whole = lambda shift: pl.BlockSpec((slot_count, PAIR), lambda h, i, *_: (0, h + shift))
    wide = jax.ShapeDtypeStruct((slot_count, D), jnp.bfloat16)
    return pl.pallas_call(
        attend_kernel,
        grid_spec=pltpu.PrefetchScalarGridSpec(
            num_scalar_prefetch=2,
            grid=(pairs, slot_count // BQ),
            in_specs=[block, whole(pairs), whole(2 * pairs)] + rope_specs + code_specs,
            out_specs=[
                block, whole(0), whole(0), block,
                pl.BlockSpec((1, 8, BQ), lambda h, i, *_: (h, 0, i)),
            ],
            scratch_shapes=[pltpu.VMEM((PAIR, slot_count), jnp.bfloat16)],
        ),
        out_shape=[wide, wide, wide, wide,
                   jax.ShapeDtypeStruct((pairs, 8, slot_count), jnp.float32)],
        compiler_params=pltpu.CompilerParams(vmem_limit_bytes=40 * 2**20),
        cost_estimate=pl.CostEstimate(
            flops=16 * slot_count * slot_count * D, bytes_accessed=24 * slot_count * D,
            transcendentals=HEADS * slot_count * slot_count),
    )(lo, width, joined, joined, joined, cosine, sine, code_row, code_col)


def attend_back(qr, kr, vr, grad_mixed, lse, tables):
    lo, width, cosine, sine, code_row, code_col = tables
    slot_count = qr.shape[0]
    pairs = D // PAIR
    rope_specs, code_specs = table_specs(slot_count)
    block = pl.BlockSpec((BQ, PAIR), lambda h, i, *_: (i, h))
    whole = pl.BlockSpec((slot_count, PAIR), lambda h, i, *_: (0, h))
    wide = jax.ShapeDtypeStruct((slot_count, D), jnp.bfloat16)
    return pl.pallas_call(
        attend_back_kernel,
        grid_spec=pltpu.PrefetchScalarGridSpec(
            num_scalar_prefetch=2,
            grid=(pairs, slot_count // BQ),
            in_specs=[block, whole, whole, block,
                      pl.BlockSpec((1, 8, BQ), lambda h, i, *_: (h, 0, i))]
            + rope_specs + code_specs,
            out_specs=[block, whole, whole],
            scratch_shapes=[
                pltpu.VMEM((PAIR, slot_count), jnp.bfloat16),
                pltpu.VMEM((slot_count, PAIR), jnp.float32),
                pltpu.VMEM((slot_count, PAIR), jnp.float32),
            ],
        ),
        out_shape=[wide, wide, wide],
        compiler_params=pltpu.CompilerParams(vmem_limit_bytes=40 * 2**20),
        cost_estimate=pl.CostEstimate(
            flops=40 * slot_count * slot_count * D, bytes_accessed=20 * slot_count * D,
            transcendentals=HEADS * slot_count * slot_count),
    )(lo, width, qr, kr, vr, grad_mixed, lse, cosine, sine, code_row, code_col)


def halving_sum(partial, order, device_count, kind):
    bits = device_count.bit_length() - 1
    me = lax.axis_index("fsdp")
    rows, cols = partial.shape[0] // device_count, partial.shape[1]
    current = partial.reshape((2,) * bits + (rows, cols))
    for bit in order:
        axis = bits - 1 - bit
        mine = (me >> bit) & 1
        keep = lax.dynamic_slice_in_dim(current, mine, 1, axis)
        send = lax.dynamic_slice_in_dim(current, 1 - mine, 1, axis).astype(kind)
        pairs = [(index, index ^ (1 << bit)) for index in range(device_count)]
        current = keep + lax.ppermute(send, "fsdp", pairs).astype(jnp.float32)
    return current.reshape(rows, cols)


def exchange_orders(device_count):
    bits = device_count.bit_length() - 1
    middle = list(range(1, bits - 1))
    turns = [middle[t:] + middle[:t] for t in range(min(3, len(middle)))] or [middle]
    ends = [bits - 1] if bits > 1 else []
    return [[0] + turn + ends for turn in turns]


def summed_to_owners(partial, device_count):
    orders = exchange_orders(device_count)
    cols = partial.shape[1] // len(orders)
    return jnp.concatenate(
        [
            halving_sum(partial[:, t * cols : (t + 1) * cols], order, device_count, jnp.bfloat16)
            for t, order in enumerate(orders)
        ],
        axis=1,
    )


def doubling_gather(block, device_count):
    me = lax.axis_index("fsdp")
    current = block
    for bit in range(device_count.bit_length() - 1):
        pairs = [(index, index ^ (1 << bit)) for index in range(device_count)]
        other = lax.ppermute(current, "fsdp", pairs)
        upper = (me >> bit) & 1 == 1
        current = jnp.concatenate(
            [jnp.where(upper, other, current), jnp.where(upper, current, other)], axis=0
        )
    return current


def gains_to_owners(gain_one, gain_two, device_count):
    own = gain_one.shape[0] // device_count
    both = jnp.stack([gain_one.reshape(device_count, own), gain_two.reshape(device_count, own)], 1)
    both = jnp.pad(both, ((0, 0), (0, 0), (0, 128 - own))).reshape(2 * device_count, 128)
    done = halving_sum(both, exchange_orders(device_count)[0], device_count, jnp.float32)
    return done[0, :own], done[1, :own]


def right_product(left, weight):
    return lax.dot_general(
        left, weight, (((1,), (1,)), ((), ())), preferred_element_type=jnp.float32
    )


def outer_sum(grads, inputs):
    return lax.dot_general(
        grads, inputs, (((0,), (0,)), ((), ())), preferred_element_type=jnp.float32
    )


def local(
    device_count,
    hidden_in,
    segment_ids,
    project_in,
    project_out,
    expand_weight,
    shrink_weight,
    first_gain,
    second_gain,
    cotangent,
):
    slot_count = hidden_in.shape[0]
    own_gain = first_gain.shape[0]
    both_gains = jnp.pad(jnp.stack([first_gain, second_gain]), ((0, 0), (0, 128 - own_gain)))
    gains = doubling_gather(both_gains[None], device_count)
    gain_one = gains[:, 0, :own_gain].reshape(device_count * own_gain)
    gain_two = gains[:, 1, :own_gain].reshape(device_count * own_gain)
    full_in = lax.all_gather(project_in, "fsdp", axis=0, tiled=True)
    full_out = lax.all_gather(project_out, "fsdp", axis=0, tiled=True)
    full_expand = lax.all_gather(expand_weight, "fsdp", axis=0, tiled=True)
    full_shrink = lax.all_gather(shrink_weight, "fsdp", axis=0, tiled=True)
    tables = attention_tables(segment_ids)
    hidden = hidden_in.astype(jnp.float32)
    normed, norm_back_one = jax.vjp(layer_norm, hidden, gain_one.astype(jnp.float32))
    normed_low = normed.astype(jnp.bfloat16)
    joined = right_product(normed_low, full_in)
    queries_low, keys_low, values_low, mixed_low, lse = attend(joined, tables)
    middle = hidden + right_product(mixed_low, full_out)
    normed_two, norm_back_two = jax.vjp(layer_norm, middle, gain_two.astype(jnp.float32))
    normed_two_low = normed_two.astype(jnp.bfloat16)
    widened = right_product(normed_two_low, full_expand)
    product, glu_back = jax.vjp(gated_gelu, widened[:, :FF], widened[:, FF:])
    product_low = product.astype(jnp.bfloat16)
    hidden_out = (middle + right_product(product_low, full_shrink)).astype(jnp.bfloat16)
    grad_shrink = outer_sum(cotangent, product_low)
    grad_product = jnp.dot(cotangent, full_shrink, preferred_element_type=jnp.float32)
    grad_gate, grad_upward = glu_back(grad_product)
    grad_wide = jnp.concatenate([grad_gate, grad_upward], axis=1).astype(jnp.bfloat16)
    grad_expand = outer_sum(grad_wide, normed_two_low)
    grad_normed_two = jnp.dot(grad_wide, full_expand, preferred_element_type=jnp.float32)
    grad_mid_norm, grad_gain_two = norm_back_two(grad_normed_two)
    grad_middle = cotangent.astype(jnp.float32) + grad_mid_norm
    grad_mid_low = grad_middle.astype(jnp.bfloat16)
    grad_project_out = outer_sum(grad_mid_low, mixed_low)
    grad_mixed = jnp.dot(grad_mid_low, full_out, preferred_element_type=jnp.float32).astype(
        jnp.bfloat16
    )
    owned_shrink = summed_to_owners(grad_shrink, device_count)
    owned_expand = summed_to_owners(grad_expand, device_count)
    owned_out = summed_to_owners(grad_project_out, device_count)
    grad_joined = jnp.concatenate(
        attend_back(queries_low, keys_low, values_low, grad_mixed, lse, tables), axis=1
    )
    grad_project_in = outer_sum(grad_joined, normed_low)
    grad_normed = jnp.dot(grad_joined, full_in, preferred_element_type=jnp.float32)
    grad_hidden_norm, grad_gain_one = norm_back_one(grad_normed)
    grad_input = (grad_middle + grad_hidden_norm).astype(jnp.bfloat16)
    owned_in = summed_to_owners(grad_project_in, device_count)
    owned_gain_one, owned_gain_two = gains_to_owners(grad_gain_one, grad_gain_two, device_count)
    return (
        hidden_out,
        grad_input,
        owned_in,
        owned_out,
        owned_expand,
        owned_shrink,
        owned_gain_one,
        owned_gain_two,
    )


def solution(mesh):
    return jax.shard_map(
        functools.partial(local, mesh.shape["fsdp"]),
        mesh=mesh,
        in_specs=(
            P("fsdp", None),
            P("fsdp"),
            P("fsdp", None),
            P("fsdp", None),
            P("fsdp", None),
            P("fsdp", None),
            P("fsdp"),
            P("fsdp"),
            P("fsdp", None),
        ),
        out_specs=(
            P("fsdp", None),
            P("fsdp", None),
            P("fsdp", None),
            P("fsdp", None),
            P("fsdp", None),
            P("fsdp", None),
            P("fsdp"),
            P("fsdp"),
        ),
        check_vma=False,
    )
```

```python
import functools

import jax
import jax.numpy as jnp
from jax import lax
from jax.experimental import pallas as pl
from jax.experimental.pallas import tpu as pltpu
from jax.sharding import PartitionSpec as P

D = 768
HEADS = 12
HEAD_DIM = 64
FF = 1152


eps_norm = 1e-05
rope_base = 160000.0
masked_score = -1e30


def layer_norm(values, gain):
    center = jnp.mean(values, axis=-1, keepdims=True)
    centred = values - center
    spread = jnp.mean(centred * centred, axis=-1, keepdims=True)
    return centred * lax.rsqrt(spread + eps_norm) * gain


def gated_gelu(gate, upward):
    return jax.nn.gelu(gate, approximate=False) * upward


BQ = 256
PAIR = 2 * HEAD_DIM
STEP = 128


def swap_halves(values):
    lane = lax.broadcasted_iota(jnp.int32, values.shape, 1)
    low_half = lane % HEAD_DIM < HEAD_DIM // 2
    up = pltpu.roll(values, PAIR - HEAD_DIM // 2, 1)
    down = pltpu.roll(values, HEAD_DIM // 2, 1)
    return jnp.where(low_half, up, down)


def dot_nt(left, right):
    return lax.dot_general(
        left, right, (((1,), (1,)), ((), ())), preferred_element_type=jnp.float32
    )


def dot_nn(left, right):
    return jnp.dot(left, right, preferred_element_type=jnp.float32)


def attend_kernel(
    lo_ref, width_ref, q_ref, k_ref, v_ref, cos_ref, sin_ref, code_row_ref, code_col_ref,
    qr_ref, kr_ref, vr_ref, mixed_ref, lse_ref, vt_ref,
):
    number = pl.program_id(1)
    total = k_ref.shape[0]

    @pl.when(number == 0)
    def _():
        keys = k_ref[...]
        kr_ref[...] = (keys * cos_ref[...] + swap_halves(keys) * sin_ref[...]).astype(jnp.bfloat16)
        vr_ref[...] = v_ref[...].astype(jnp.bfloat16)
        vt_ref[...] = v_ref[...].T.astype(jnp.bfloat16)

    rows = pl.ds(pl.multiple_of(number * BQ, BQ), BQ)
    queries = q_ref[...]
    queries = queries * cos_ref[rows, :] + swap_halves(queries) * sin_ref[rows, :]
    queries = queries.astype(jnp.bfloat16) * jnp.bfloat16(HEAD_DIM**-0.5)
    qr_ref[...] = queries
    start = pl.multiple_of(lo_ref[number] * STEP, STEP)

    for quarter in range(1, total // BQ + 1):
        width = quarter * BQ

        @pl.when(width_ref[number] == quarter)
        def _():
            window = pl.ds(start, width)
            allowed = code_col_ref[window, :1] == code_row_ref[:1, :]
            outs = []
            for side in range(2):
                part = slice(side * HEAD_DIM, (side + 1) * HEAD_DIM)
                scores = dot_nt(kr_ref[window, part], queries[:, part])
                scores = jnp.where(allowed, scores, masked_score)
                peak = jnp.max(scores, axis=0, keepdims=True)
                shifted = jnp.exp(scores - peak)
                amount = jnp.sum(shifted, axis=0, keepdims=True)
                lse_ref[0, side : side + 1, :] = peak + jnp.log(amount)
                out = dot_nn(vt_ref[part, window], shifted.astype(jnp.bfloat16))
                outs.append(out * (1.0 / amount))
            mixed_ref[...] = jnp.concatenate(outs, axis=0).T.astype(jnp.bfloat16)


def attend_back_kernel(
    lo_ref, width_ref, qr_ref, kr_ref, vr_ref, gm_ref, lse_ref, cos_ref, sin_ref,
    code_row_ref, code_col_ref, gq_ref, gk_ref, gv_ref, kt_ref, gk_sum, gv_sum,
):
    number = pl.program_id(1)
    total = kr_ref.shape[0]

    @pl.when(number == 0)
    def _():
        kt_ref[...] = kr_ref[...].astype(jnp.float32).T.astype(jnp.bfloat16)
        gk_sum[...] = jnp.zeros_like(gk_sum)
        gv_sum[...] = jnp.zeros_like(gv_sum)

    rows = pl.ds(pl.multiple_of(number * BQ, BQ), BQ)
    queries = qr_ref[...]
    grads = gm_ref[...]
    start = pl.multiple_of(lo_ref[number] * STEP, STEP)

    for quarter in range(1, total // BQ + 1):
        width = quarter * BQ

        @pl.when(width_ref[number] == quarter)
        def _():
            window = pl.ds(start, width)
            allowed = code_col_ref[window, :1] == code_row_ref[:1, :]
            outs, key_parts, value_parts = [], [], []
            for side in range(2):
                part = slice(side * HEAD_DIM, (side + 1) * HEAD_DIM)
                scores = dot_nt(kr_ref[window, part], queries[:, part])
                scores = jnp.where(allowed, scores, masked_score)
                probs = jnp.exp(scores - lse_ref[0, side : side + 1, :])
                value_parts.append(dot_nn(probs.astype(jnp.bfloat16), grads[:, part]))
                weighted = probs * dot_nt(vr_ref[window, part], grads[:, part])
                row_dot = jnp.sum(weighted, axis=0, keepdims=True)
                grad_scores = (weighted - probs * row_dot).astype(jnp.bfloat16)
                key_parts.append(dot_nn(grad_scores, queries[:, part]))
                outs.append(dot_nn(kt_ref[part, window], grad_scores))
            gv_sum[window, :] += jnp.concatenate(value_parts, axis=1)
            gk_sum[window, :] += jnp.concatenate(key_parts, axis=1)
            out = jnp.concatenate(outs, axis=0).T * HEAD_DIM**-0.5
            gq_ref[...] = (
                out * cos_ref[rows, :] - swap_halves(out) * sin_ref[rows, :]
            ).astype(jnp.bfloat16)

    @pl.when(number == pl.num_programs(1) - 1)
    def _():
        keys = gk_sum[...]
        gk_ref[...] = (keys * cos_ref[...] - swap_halves(keys) * sin_ref[...]).astype(jnp.bfloat16)
        gv_ref[...] = gv_sum[...].astype(jnp.bfloat16)


def attention_tables(segment_ids):
    slot_count = segment_ids.shape[0]
    slots = jnp.arange(slot_count, dtype=jnp.int32)
    same = segment_ids[:, None] == segment_ids[None, :]
    starts = jnp.min(jnp.where(same, slots[None, :], slot_count), axis=1)
    ends = jnp.max(jnp.where(same, slots[None, :], -1), axis=1) + 1
    padding = segment_ids < 0
    code = jnp.where(padding, -1 - slots, segment_ids)
    first = jnp.where(padding, slots, starts)[::BQ] // STEP
    last = (jnp.where(padding, slots + 1, ends)[BQ - 1 :: BQ] + STEP - 1) // STEP
    ratio = BQ // STEP
    width = (last - first + ratio - 1) // ratio
    lo = jnp.minimum(first, slot_count // STEP - ratio * width)
    position = (slots - starts).astype(jnp.float32)
    lane = jnp.arange(PAIR, dtype=jnp.int32)
    half = HEAD_DIM // 2
    freq = rope_base ** (-(lane % half).astype(jnp.float32) * 2.0 / HEAD_DIM)
    angle = position[:, None] * freq[None, :]
    sign = jnp.where(lane % HEAD_DIM < half, -1.0, 1.0)
    code_row = jnp.broadcast_to(code[None, :], (8, slot_count))
    code_col = jnp.broadcast_to(code[:, None], (slot_count, STEP))
    return lo, width, jnp.cos(angle), jnp.sin(angle) * sign[None, :], code_row, code_col


def table_specs(slot_count):
    return (
        [pl.BlockSpec((slot_count, PAIR), lambda h, i, *_: (0, 0))] * 2,
        [
            pl.BlockSpec((8, BQ), lambda h, i, *_: (0, i)),
            pl.BlockSpec((slot_count, STEP), lambda h, i, *_: (0, 0)),
        ],
    )


def attend(joined, tables):
    lo, width, cosine, sine, code_row, code_col = tables
    slot_count = joined.shape[0]
    pairs = D // PAIR
    rope_specs, code_specs = table_specs(slot_count)
    block = pl.BlockSpec((BQ, PAIR), lambda h, i, *_: (i, h))
    whole = lambda shift: pl.BlockSpec((slot_count, PAIR), lambda h, i, *_: (0, h + shift))
    wide = jax.ShapeDtypeStruct((slot_count, D), jnp.bfloat16)
    return pl.pallas_call(
        attend_kernel,
        grid_spec=pltpu.PrefetchScalarGridSpec(
            num_scalar_prefetch=2,
            grid=(pairs, slot_count // BQ),
            in_specs=[block, whole(pairs), whole(2 * pairs)] + rope_specs + code_specs,
            out_specs=[
                block, whole(0), whole(0), block,
                pl.BlockSpec((1, 8, BQ), lambda h, i, *_: (h, 0, i)),
            ],
            scratch_shapes=[pltpu.VMEM((PAIR, slot_count), jnp.bfloat16)],
        ),
        out_shape=[wide, wide, wide, wide,
                   jax.ShapeDtypeStruct((pairs, 8, slot_count), jnp.float32)],
        compiler_params=pltpu.CompilerParams(vmem_limit_bytes=40 * 2**20),
        cost_estimate=pl.CostEstimate(
            flops=16 * slot_count * slot_count * D, bytes_accessed=24 * slot_count * D,
            transcendentals=HEADS * slot_count * slot_count),
    )(lo, width, joined, joined, joined, cosine, sine, code_row, code_col)


def attend_back(qr, kr, vr, grad_mixed, lse, tables):
    lo, width, cosine, sine, code_row, code_col = tables
    slot_count = qr.shape[0]
    pairs = D // PAIR
    rope_specs, code_specs = table_specs(slot_count)
    block = pl.BlockSpec((BQ, PAIR), lambda h, i, *_: (i, h))
    whole = pl.BlockSpec((slot_count, PAIR), lambda h, i, *_: (0, h))
    wide = jax.ShapeDtypeStruct((slot_count, D), jnp.bfloat16)
    return pl.pallas_call(
        attend_back_kernel,
        grid_spec=pltpu.PrefetchScalarGridSpec(
            num_scalar_prefetch=2,
            grid=(pairs, slot_count // BQ),
            in_specs=[block, whole, whole, block,
                      pl.BlockSpec((1, 8, BQ), lambda h, i, *_: (h, 0, i))]
            + rope_specs + code_specs,
            out_specs=[block, whole, whole],
            scratch_shapes=[
                pltpu.VMEM((PAIR, slot_count), jnp.bfloat16),
                pltpu.VMEM((slot_count, PAIR), jnp.float32),
                pltpu.VMEM((slot_count, PAIR), jnp.float32),
            ],
        ),
        out_shape=[wide, wide, wide],
        compiler_params=pltpu.CompilerParams(vmem_limit_bytes=40 * 2**20),
        cost_estimate=pl.CostEstimate(
            flops=40 * slot_count * slot_count * D, bytes_accessed=20 * slot_count * D,
            transcendentals=HEADS * slot_count * slot_count),
    )(lo, width, qr, kr, vr, grad_mixed, lse, cosine, sine, code_row, code_col)


def halving_sum(partial, order, device_count, kind):
    bits = device_count.bit_length() - 1
    me = lax.axis_index("fsdp")
    rows, cols = partial.shape[0] // device_count, partial.shape[1]
    current = partial.reshape((2,) * bits + (rows, cols))
    for bit in order:
        axis = bits - 1 - bit
        mine = (me >> bit) & 1
        keep = lax.dynamic_slice_in_dim(current, mine, 1, axis)
        send = lax.dynamic_slice_in_dim(current, 1 - mine, 1, axis).astype(kind)
        pairs = [(index, index ^ (1 << bit)) for index in range(device_count)]
        current = keep + lax.ppermute(send, "fsdp", pairs).astype(jnp.float32)
    return current.reshape(rows, cols)


def exchange_orders(device_count):
    bits = device_count.bit_length() - 1
    middle = list(range(1, bits - 1))
    turns = [middle[t:] + middle[:t] for t in range(min(3, len(middle)))] or [middle]
    ends = [bits - 1] if bits > 1 else []
    return [[0] + turn + ends for turn in turns]


def summed_to_owners(partial, device_count):
    orders = exchange_orders(device_count)
    cols = partial.shape[1] // len(orders)
    return jnp.concatenate(
        [
            halving_sum(partial[:, t * cols : (t + 1) * cols], order, device_count, jnp.bfloat16)
            for t, order in enumerate(orders)
        ],
        axis=1,
    )


def doubling_gather(block, device_count):
    me = lax.axis_index("fsdp")
    bits = device_count.bit_length() - 1
    current = block[0]
    for stage in range(bits):
        bit = bits - 1 - stage
        pairs = [(index, index ^ (1 << bit)) for index in range(device_count)]
        other = lax.ppermute(current, "fsdp", pairs)
        upper = (me >> bit) & 1 == 1
        current = jnp.stack(
            [jnp.where(upper, other, current), jnp.where(upper, current, other)], axis=stage
        )
    return current.reshape((device_count,) + block.shape[1:])


def full_rows(block, device_count):
    gathered = doubling_gather(block[None], device_count)
    return gathered.reshape(device_count * block.shape[0], block.shape[1])


def gains_to_owners(gain_one, gain_two, device_count):
    own = gain_one.shape[0] // device_count
    both = jnp.stack([gain_one.reshape(device_count, own), gain_two.reshape(device_count, own)], 1)
    both = jnp.pad(both, ((0, 0), (0, 0), (0, 128 - own))).reshape(2 * device_count, 128)
    done = halving_sum(both, exchange_orders(device_count)[0], device_count, jnp.float32)
    return done[0, :own], done[1, :own]


def right_product(left, weight):
    return lax.dot_general(
        left, weight, (((1,), (1,)), ((), ())), preferred_element_type=jnp.float32
    )


def outer_sum(grads, inputs):
    return lax.dot_general(
        grads, inputs, (((0,), (0,)), ((), ())), preferred_element_type=jnp.float32
    )


def local(
    device_count,
    hidden_in,
    segment_ids,
    project_in,
    project_out,
    expand_weight,
    shrink_weight,
    first_gain,
    second_gain,
    cotangent,
):
    slot_count = hidden_in.shape[0]
    own_gain = first_gain.shape[0]
    both_gains = jnp.pad(jnp.stack([first_gain, second_gain]), ((0, 0), (0, 128 - own_gain)))
    gains = doubling_gather(both_gains[None], device_count)
    gain_one = gains[:, 0, :own_gain].reshape(device_count * own_gain)
    gain_two = gains[:, 1, :own_gain].reshape(device_count * own_gain)
    full_in = full_rows(project_in, device_count)
    full_out = full_rows(project_out, device_count)
    full_expand = full_rows(expand_weight, device_count)
    full_shrink = full_rows(shrink_weight, device_count)
    tables = attention_tables(segment_ids)
    hidden = hidden_in.astype(jnp.float32)
    normed, norm_back_one = jax.vjp(layer_norm, hidden, gain_one.astype(jnp.float32))
    normed_low = normed.astype(jnp.bfloat16)
    joined = right_product(normed_low, full_in)
    queries_low, keys_low, values_low, mixed_low, lse = attend(joined, tables)
    middle = hidden + right_product(mixed_low, full_out)
    normed_two, norm_back_two = jax.vjp(layer_norm, middle, gain_two.astype(jnp.float32))
    normed_two_low = normed_two.astype(jnp.bfloat16)
    widened = right_product(normed_two_low, full_expand)
    product, glu_back = jax.vjp(gated_gelu, widened[:, :FF], widened[:, FF:])
    product_low = product.astype(jnp.bfloat16)
    hidden_out = (middle + right_product(product_low, full_shrink)).astype(jnp.bfloat16)
    grad_shrink = outer_sum(cotangent, product_low)
    grad_product = jnp.dot(cotangent, full_shrink, preferred_element_type=jnp.float32)
    grad_gate, grad_upward = glu_back(grad_product)
    grad_wide = jnp.concatenate([grad_gate, grad_upward], axis=1).astype(jnp.bfloat16)
    grad_expand = outer_sum(grad_wide, normed_two_low)
    grad_normed_two = jnp.dot(grad_wide, full_expand, preferred_element_type=jnp.float32)
    grad_mid_norm, grad_gain_two = norm_back_two(grad_normed_two)
    grad_middle = cotangent.astype(jnp.float32) + grad_mid_norm
    grad_mid_low = grad_middle.astype(jnp.bfloat16)
    grad_project_out = outer_sum(grad_mid_low, mixed_low)
    grad_mixed = jnp.dot(grad_mid_low, full_out, preferred_element_type=jnp.float32).astype(
        jnp.bfloat16
    )
    owned_shrink = summed_to_owners(grad_shrink, device_count)
    owned_expand = summed_to_owners(grad_expand, device_count)
    owned_out = summed_to_owners(grad_project_out, device_count)
    grad_joined = jnp.concatenate(
        attend_back(queries_low, keys_low, values_low, grad_mixed, lse, tables), axis=1
    )
    grad_project_in = outer_sum(grad_joined, normed_low)
    grad_normed = jnp.dot(grad_joined, full_in, preferred_element_type=jnp.float32)
    grad_hidden_norm, grad_gain_one = norm_back_one(grad_normed)
    grad_input = (grad_middle + grad_hidden_norm).astype(jnp.bfloat16)
    owned_in = summed_to_owners(grad_project_in, device_count)
    owned_gain_one, owned_gain_two = gains_to_owners(grad_gain_one, grad_gain_two, device_count)
    return (
        hidden_out,
        grad_input,
        owned_in,
        owned_out,
        owned_expand,
        owned_shrink,
        owned_gain_one,
        owned_gain_two,
    )


def solution(mesh):
    return jax.shard_map(
        functools.partial(local, mesh.shape["fsdp"]),
        mesh=mesh,
        in_specs=(
            P("fsdp", None),
            P("fsdp"),
            P("fsdp", None),
            P("fsdp", None),
            P("fsdp", None),
            P("fsdp", None),
            P("fsdp"),
            P("fsdp"),
            P("fsdp", None),
        ),
        out_specs=(
            P("fsdp", None),
            P("fsdp", None),
            P("fsdp", None),
            P("fsdp", None),
            P("fsdp", None),
            P("fsdp", None),
            P("fsdp"),
            P("fsdp"),
        ),
        check_vma=False,
    )
```
